32 devices in a mesh: src: 4 (over y, core), snk: 8 (over z, x).
Axes of the slice: x: 2, y: 2, z: 4, core: 2. Of those that a mesh axis runs over, the one named last changes fastest.
Arguments:
- peram: bfloat16 [4, 8, 2, 256, 256], P('src', None, None, None, 'snk'), may hold values from -6 to 6
- meson_blocks: bfloat16 [8, 4, 2, 256, 256], P('snk'), may hold values from -0.25 to 0.25
- edge_left: int32 [4, 8, 32], P('src', 'snk'), may hold values from 0 to 3
- edge_right: int32 [4, 8, 32], P('src', 'snk'), may hold values from 0 to 3
- edge_node: int32 [4, 8, 32], P('src', 'snk'), may hold values from 0 to 4
- edge_weight: int32 [4, 8, 32], P('src', 'snk'), may hold values from 0 to 15
- weight_table: float32 [16, 2], replicated, may hold values from -0.2 to 0.2
Outputs:
- node_matrices: bfloat16 [256, 4, 2, 256], P('snk')
The draws below stay inside these ranges and needn't reach their ends.
Inputs may be any that keep to these rules, and one draw needn't show every extreme that they name: `edge_node`: the value 4 marks an empty slot that feeds no node.
All inputs are finite; a program needn't handle non-finite values.
Results may differ from the reference program's by a relative error of at most 0.009.
Values may be sent and summed in bfloat16 or wider, within the bound.
A program may use at most 128 MiB of HBM per device.

```python
import jax
import jax.numpy as jnp
from jax import lax

N = 256
MOM = 4
E_DEV = 32
NODES = 4
NW = 16
NS = 4
NT = 8
N_SRC = 4
N_SNK = 8


def with_ends(drawn, stream_key, least, largest):
    place = [jax.random.randint(jax.random.fold_in(stream_key, axis), (), 0, length) for axis, length in enumerate(drawn.shape)]
    widest = drawn.shape.index(max(drawn.shape))
    beside = place[:widest] + [(place[widest] + 1) % drawn.shape[widest]] + place[widest + 1:]
    return drawn.at[tuple(place)].set(least).at[tuple(beside)].set(largest)


def block_levels(own_key, extent, pieces, smallest, top_value):
    def one(position, blocks):
        draws = jax.random.uniform(jax.random.fold_in(jax.random.fold_in(own_key, 6), position), (blocks,), jnp.float32, smallest / len(pieces), top_value / len(pieces))
        return jnp.repeat(jnp.exp(draws), extent[position] // blocks).reshape((-1,) + (1,) * (len(extent) - position - 1))

    gain = one(*pieces[0])
    for cut in pieces[1:]:
        gain = gain * one(*cut)
    return gain


def scatter_about(own_key, extent, width, reach, pieces=(), kind=jnp.bfloat16):
    entries = width * jax.random.normal(own_key, extent, jnp.float32)
    if pieces:
        entries = entries * block_levels(own_key, extent, pieces, -0.22, 0.18)
    return jnp.clip(entries, -reach, reach).astype(kind)


def setup_inputs(seed: int = 0) -> dict:
    seeds = jax.random.split(jax.random.key(seed), 8)
    peram = scatter_about(seeds[0], (NS, NT, 2, N, N), 1.0, 6.0, ((0, 4), (4, 8)))
    meson_blocks = scatter_about(seeds[1], (NT, MOM, 2, N, N), (2 * N) ** -0.5, 0.25, ((0, 8),))
    edge_left = with_ends(jax.random.randint(seeds[2], (NS, NT, E_DEV), 0, MOM), jax.random.fold_in(seeds[2], 1), 0, MOM - 1).astype(jnp.int32)
    edge_right = with_ends(jax.random.randint(seeds[3], (NS, NT, E_DEV), 0, MOM), jax.random.fold_in(seeds[3], 1), 0, MOM - 1).astype(jnp.int32)
    edge_node = with_ends(jax.random.randint(seeds[4], (NS, NT, E_DEV), 0, NODES + 1), jax.random.fold_in(seeds[4], 1), 0, NODES).astype(jnp.int32)
    edge_weight = with_ends(jax.random.randint(seeds[5], (NS, NT, E_DEV), 0, NW), jax.random.fold_in(seeds[5], 1), 0, NW - 1).astype(jnp.int32)
    weight_table = scatter_about(seeds[6], (NW, 2), 0.03, 0.2, (), jnp.float32)
    return dict(peram=peram, meson_blocks=meson_blocks, edge_left=edge_left, edge_right=edge_right, edge_node=edge_node, edge_weight=edge_weight, weight_table=weight_table)


def block_products(blocks, whole_peram):
    number = blocks.shape[0]
    order = blocks.shape[2]
    left_real = blocks[:, 0].reshape(number * order, order)
    left_imag = blocks[:, 1].reshape(number * order, order)
    real_part = jnp.dot(left_real, whole_peram[0], preferred_element_type=jnp.float32) - jnp.dot(left_imag, whole_peram[1], preferred_element_type=jnp.float32)
    imag_part = jnp.dot(left_real, whole_peram[1], preferred_element_type=jnp.float32) + jnp.dot(left_imag, whole_peram[0], preferred_element_type=jnp.float32)
    stacked = jnp.stack([real_part.reshape(number, order, order), imag_part.reshape(number, order, order)], 1)
    return stacked.astype(jnp.bfloat16)


def reference(peram, meson_blocks, edge_left, edge_right, edge_node, edge_weight, weight_table):
    high = lax.Precision.HIGHEST
    time_stride = N_SNK // N_SRC
    node_ids = jnp.arange(NODES, dtype=jnp.int32)
    block_ids = jnp.arange(MOM, dtype=jnp.int32)
    table_ids = jnp.arange(NW, dtype=jnp.int32)

    def one_time(running, inputs):
        whole_peram, blocks, left_of, right_of, node_of, weight_of = inputs
        left_times = block_products(blocks, whole_peram).astype(jnp.float32)
        pick_weight = (weight_of[:, None] == table_ids[None, :]).astype(jnp.float32)
        edge_coef = jnp.dot(pick_weight, weight_table, precision=high)
        member = (node_of[:, None] == node_ids[None, :]).astype(jnp.float32)
        pick_right = (right_of[:, None] == block_ids[None, :]).astype(jnp.float32)
        pick_left = (left_of[:, None] == block_ids[None, :]).astype(jnp.float32)
        mix_real = jnp.einsum("en,eb,ea->nba", member * edge_coef[:, 0:1], pick_right, pick_left, precision=high)
        mix_imag = jnp.einsum("en,eb,ea->nba", member * edge_coef[:, 1:2], pick_right, pick_left, precision=high)
        pair_real = jnp.einsum("nba,aij->nbij", mix_real, left_times[:, 0], precision=high) - jnp.einsum("nba,aij->nbij", mix_imag, left_times[:, 1], precision=high)
        pair_imag = jnp.einsum("nba,aij->nbij", mix_real, left_times[:, 1], precision=high) + jnp.einsum("nba,aij->nbij", mix_imag, left_times[:, 0], precision=high)
        return (running[0] + pair_real, running[1] + pair_imag), None

    def one_source(inputs):
        source_index, peram_s, left_s, right_s, node_s, weight_s = inputs
        empty_sums = jnp.zeros((NODES, MOM, N, N), jnp.float32)
        sums, unused = lax.scan(one_time, (empty_sums, empty_sums), (peram_s, meson_blocks, left_s, right_s, node_s, weight_s))
        right_f = lax.dynamic_index_in_dim(meson_blocks, (source_index * time_stride).astype(jnp.int32), 0, keepdims=False).astype(jnp.float32)
        out_real = jnp.einsum("nbij,bjk->nik", sums[0], right_f[:, 0], precision=high) - jnp.einsum("nbij,bjk->nik", sums[1], right_f[:, 1], precision=high)
        out_imag = jnp.einsum("nbij,bjk->nik", sums[0], right_f[:, 1], precision=high) + jnp.einsum("nbij,bjk->nik", sums[1], right_f[:, 0], precision=high)
        return jnp.stack([out_real, out_imag], 1)

    per_source = lax.map(one_source, (jnp.arange(N_SRC, dtype=jnp.int32), peram, edge_left, edge_right, edge_node, edge_weight))
    summed = jnp.sum(per_source, axis=0)
    return jnp.transpose(summed, (2, 0, 1, 3)).astype(jnp.bfloat16)
```

```python
import functools

import jax
import jax.numpy as jnp
from jax import lax
from jax.experimental import pallas as pl
from jax.experimental.pallas import tpu as pltpu
from jax.sharding import PartitionSpec as P

NODES = 4
NW = 16
MESH = pl.DeviceIdType.MESH
F32 = jnp.float32
BF16 = jnp.bfloat16
MIX_ROWS = 16


def kernel(
    n_src, n_snk, mom, order,
    tau_ref, blocks_ref, left_ref, right_ref, node_ref, weight_ref, table_ref,
    out_ref,
    tau_in, right_buf, coef, mixed, tau_cat, prod, part, part_in, share, share_in, done,
    tau_send, tau_recv, cast_send, cast_recv, part_send, part_recv, share_send, share_recv, done_send, done_recv,
):
    s = lax.axis_index("src")
    t = lax.axis_index("snk")
    planes = NODES * 2 // n_src
    rows = order // n_snk
    half = mom
    root = s * (n_snk // n_src)
    high, low = t // 2, t % 2
    root_high, root_low = root // 2, root % 2
    other = 1 - low
    is_root = t == root
    pair_is_root = (high == root_high) & (other == root_low)
    goes_up = (high >= root_high) & (high + 1 < n_snk // 2)
    goes_down = (high <= root_high) & (high >= 1)

    def snk_peer(d):
        return lax.rem(t + d, n_snk)

    def src_peer(d):
        return lax.rem(s + d, n_src)

    barrier = pltpu.get_barrier_semaphore()
    for d in range(1, n_snk):
        pl.semaphore_signal(barrier, inc=1, device_id=(s, snk_peer(d)), device_id_type=MESH)
    for d in range(1, n_src):
        pl.semaphore_signal(barrier, inc=1, device_id=(src_peer(d), t), device_id_type=MESH)
    pl.semaphore_wait(barrier, n_snk + n_src - 2)

    def cast(piece, kind, q, target):
        return pltpu.make_async_remote_copy(
            src_ref=right_buf.at[piece], dst_ref=right_buf.at[piece],
            send_sem=cast_send.at[kind, q], recv_sem=cast_recv.at[piece],
            device_id=(s, target), device_id_type=MESH,
        )

    def cast_ways(q):
        mine = low * half + q
        return (
            (goes_up, cast(mine, 0, q, jnp.minimum(t + 2, n_snk - 1))),
            (goes_down, cast(mine, 1, q, jnp.maximum(t - 2, 0))),
            (jnp.logical_not(pair_is_root), cast(mine, 2, q, high * 2 + other)),
        )

    def cast_rest(q):
        return cast(other * half + q, 3, q, high * 2 + other)

    def cast_arrived(piece):
        @pl.when(jnp.logical_not(is_root))
        def _():
            cast(piece, 0, 0, high * 2 + other).wait_recv()

    @pl.when(is_root)
    def _():
        for piece in range(2 * mom):
            right_buf[piece] = blocks_ref[piece]
        for q in range(half):
            cast_rest(q).start()

    tau_copies = []
    for d in range(1, n_snk):
        copy = pltpu.make_async_remote_copy(
            src_ref=tau_ref.at[snk_peer(d)], dst_ref=tau_in.at[t],
            send_sem=tau_send.at[d - 1], recv_sem=tau_recv.at[d - 1],
            device_id=(s, snk_peer(d)), device_id_type=MESH,
        )
        copy.start()
        tau_copies.append(copy)
    tau_in[t] = tau_ref[t]

    table_row = lax.broadcasted_iota(jnp.int32, (NW, 1), 0)
    picks = table_row == weight_ref[...]
    slot = (node_ref[...] * mom + right_ref[...]) * mom + left_ref[...]
    slots = NODES * mom * mom
    feeds = lax.broadcasted_iota(jnp.int32, (slots, 1), 0) == slot
    for c in range(2):
        gain = jnp.sum(jnp.where(picks, table_ref[:, c : c + 1], 0.0), axis=0, keepdims=True)
        total = jnp.sum(jnp.where(feeds, gain, 0.0), axis=1, keepdims=True)
        coef[c] = jnp.broadcast_to(total, (slots, order))

    def mix_node(n):
        def step(i, carry):
            span = pl.ds(pl.multiple_of(i * MIX_ROWS, MIX_ROWS), MIX_ROWS)
            real = [blocks_ref[2 * a, span, :].astype(F32) for a in range(mom)]
            imag = [blocks_ref[2 * a + 1, span, :].astype(F32) for a in range(mom)]
            for b in range(mom):
                sum_real = sum_imag = 0.0
                for a in range(mom):
                    k = (n * mom + b) * mom + a
                    gain_real, gain_imag = coef[0, k : k + 1, :], coef[1, k : k + 1, :]
                    sum_real += gain_real * real[a] - gain_imag * imag[a]
                    sum_imag += gain_real * imag[a] + gain_imag * real[a]
                at = 2 * b * order
                mixed[n, span, at : at + order] = sum_real.astype(BF16)
                mixed[n, span, at + order : at + 2 * order] = sum_imag.astype(BF16)
            return carry

        lax.fori_loop(0, order // MIX_ROWS, step, 0)

    with jax.named_scope("relay_and_mix"):
        for q in range(max(half, NODES)):
            if q < half:
                cast_arrived(low * half + q)
                for taken, copy in cast_ways(q):
                    pl.when(taken)(copy.start)
            if q < NODES:
                mix_node(q)

    with jax.named_scope("tau"):
        for copy in tau_copies:
            copy.wait_recv()
        whole = tau_in[...].astype(F32)
        tau_real = whole[:, 0].reshape(order, order).T
        tau_imag = whole[:, 1].reshape(order, order).T
        tau_cat[:order, :order] = tau_real.astype(BF16)
        tau_cat[:order, order:] = (-tau_imag).astype(BF16)
        tau_cat[order:, :order] = tau_imag.astype(BF16)
        tau_cat[order:, order:] = tau_real.astype(BF16)

    with jax.named_scope("times_right"):
        for j in range(mom):
            if 2 * j < mom:
                b = low * (mom // 2) + j
            else:
                b = other * (mom // 2) + j - mom // 2
                cast_arrived(2 * b)
                cast_arrived(2 * b + 1)
            right = right_buf[pl.ds(2 * b, 2)].reshape(2 * order, order)
            both = jnp.dot(tau_cat[...], right, preferred_element_type=F32)
            prod[0, b, :order] = both[:order].astype(BF16)
            prod[0, b, order:] = (-both[order:]).astype(BF16)
            prod[1, b, :order] = both[order:].astype(BF16)
            prod[1, b, order:] = both[:order].astype(BF16)

    def plane_of(p):
        return jnp.dot(
            mixed[p // 2], prod[p % 2].reshape(2 * mom * order, order), preferred_element_type=F32
        )

    part_copies = []
    with jax.named_scope("nodes"):
        for d in range(1, n_src):
            for q in range(planes):
                part[d - 1, q] = plane_of(src_peer(d) * planes + q).astype(BF16)
            copy = pltpu.make_async_remote_copy(
                src_ref=part.at[d - 1], dst_ref=part_in.at[d - 1],
                send_sem=part_send.at[d - 1], recv_sem=part_recv.at[d - 1],
                device_id=(src_peer(d), t), device_id_type=MESH,
            )
            copy.start()
            part_copies.append(copy)
        own = [plane_of(s * planes + q) for q in range(planes)]

    with jax.named_scope("sum_src"):
        for copy in part_copies:
            copy.wait_recv()
        for q in range(planes):
            total = own[q]
            for d in range(1, n_src):
                total += part_in[d - 1, q].astype(F32)
            for k in range(n_snk):
                share[k, q] = total[k * rows : (k + 1) * rows].astype(BF16)

    with jax.named_scope("sum_snk"):
        share_copies = []
        for d in range(1, n_snk):
            copy = pltpu.make_async_remote_copy(
                src_ref=share.at[snk_peer(d)], dst_ref=share_in.at[d - 1],
                send_sem=share_send.at[d - 1], recv_sem=share_recv.at[d - 1],
                device_id=(s, snk_peer(d)), device_id_type=MESH,
            )
            copy.start()
            share_copies.append(copy)
        total = share[t].astype(F32)
        for d in range(1, n_snk):
            share_copies[d - 1].wait_recv()
            total += share_in[d - 1].astype(F32)
        done[s] = total.astype(BF16)

    with jax.named_scope("spread"):
        done_copies = []
        for d in range(1, n_src):
            copy = pltpu.make_async_remote_copy(
                src_ref=done.at[s], dst_ref=done.at[s],
                send_sem=done_send.at[d - 1], recv_sem=done_recv.at[d - 1],
                device_id=(src_peer(d), t), device_id_type=MESH,
            )
            copy.start()
            done_copies.append(copy)
        for copy in done_copies:
            copy.wait_recv()
        out_ref[...] = done[...]

    for q in range(half):
        for taken, copy in cast_ways(q):
            pl.when(taken)(copy.wait_send)
        pl.when(is_root)(cast_rest(q).wait_send)
    for copy in tau_copies + part_copies + share_copies + done_copies:
        copy.wait_send()


def shards(peram, meson_blocks, edge_left, edge_right, edge_node, edge_weight, weight_table):
    n_src, n_snk = lax.axis_size("src"), lax.axis_size("snk")
    mom, order = meson_blocks.shape[1], meson_blocks.shape[3]
    rows, planes = order // n_snk, NODES * 2 // n_src
    tau = jnp.swapaxes(peram[0], 2, 3)
    blocks = meson_blocks.reshape(2 * mom, order, order)
    edges = [e.reshape(1, -1) for e in (edge_left, edge_right, edge_node, edge_weight)]
    dma = pltpu.SemaphoreType.DMA
    out = pl.pallas_call(
        functools.partial(kernel, n_src, n_snk, mom, order),
        out_shape=jax.ShapeDtypeStruct((n_src, planes, rows, order), BF16),
        in_specs=[pl.BlockSpec(memory_space=pltpu.VMEM)] * 7,
        out_specs=pl.BlockSpec(memory_space=pltpu.VMEM),
        scratch_shapes=[
            pltpu.VMEM((n_snk, 2, rows, order), BF16),
            pltpu.VMEM((2 * mom, order, order), BF16),
            pltpu.VMEM((2, NODES * mom * mom, order), F32),
            pltpu.VMEM((NODES, order, 2 * mom * order), BF16),
            pltpu.VMEM((2 * order, 2 * order), BF16),
            pltpu.VMEM((2, mom, 2 * order, order), BF16),
            pltpu.VMEM((n_src - 1, planes, order, order), BF16),
            pltpu.VMEM((n_src - 1, planes, order, order), BF16),
            pltpu.VMEM((n_snk, planes, rows, order), BF16),
            pltpu.VMEM((n_snk - 1, planes, rows, order), BF16),
            pltpu.VMEM((n_src, planes, rows, order), BF16),
            dma((n_snk - 1,)), dma((n_snk - 1,)),
            dma((4, mom)), dma((2 * mom,)),
            dma((n_src - 1,)), dma((n_src - 1,)),
            dma((n_snk - 1,)), dma((n_snk - 1,)),
            dma((n_src - 1,)), dma((n_src - 1,)),
        ],
        compiler_params=pltpu.CompilerParams(
            collective_id=0, has_side_effects=True, vmem_limit_bytes=40 * 2**20
        ),
    )(tau, blocks, *edges, weight_table)
    out = out.reshape(NODES, 2, rows, order)
    return jnp.transpose(out, (2, 0, 1, 3))


def solution(mesh):
    return jax.shard_map(
        shards,
        mesh=mesh,
        in_specs=(
            P("src", None, None, None, "snk"),
            P("snk", None, None, None, None),
            P("src", "snk", None),
            P("src", "snk", None),
            P("src", "snk", None),
            P("src", "snk", None),
            P(),
        ),
        out_specs=P("snk", None, None, None),
        check_vma=False,
    )
```

```python
import functools

import jax
import jax.numpy as jnp
from jax import lax
from jax.experimental import pallas as pl
from jax.experimental.pallas import tpu as pltpu
from jax.sharding import PartitionSpec as P

NODES = 4
NW = 16
MESH = pl.DeviceIdType.MESH
F32 = jnp.float32
BF16 = jnp.bfloat16
MIX_ROWS = 16
SPLIT = 4


def kernel(
    n_src, n_snk, mom, order,
    tau_ref, blocks_ref, left_ref, right_ref, node_ref, weight_ref, table_ref,
    out_ref,
    tau_in, right_buf, coef, mixed, tau_cat, prod, part, part_in, share, share_in, done,
    tau_send, tau_recv, cast_send, cast_recv, part_send, part_recv, share_send, share_recv, done_send, done_recv,
):
    s = lax.axis_index("src")
    t = lax.axis_index("snk")
    planes = NODES * 2 // n_src
    rows = order // n_snk
    half = mom * SPLIT
    cut = order // SPLIT
    root = s * (n_snk // n_src)
    high, low = t // 2, t % 2
    root_high, root_low = root // 2, root % 2
    other = 1 - low
    is_root = t == root
    pair_is_root = (high == root_high) & (other == root_low)
    goes_up = (high >= root_high) & (high + 1 < n_snk // 2)
    goes_down = (high <= root_high) & (high >= 1)

    def snk_peer(d):
        return lax.rem(t + d, n_snk)

    def src_peer(d):
        return lax.rem(s + d, n_src)

    barrier = pltpu.get_barrier_semaphore()
    for d in range(1, n_snk):
        pl.semaphore_signal(barrier, inc=1, device_id=(s, snk_peer(d)), device_id_type=MESH)
    for d in range(1, n_src):
        pl.semaphore_signal(barrier, inc=1, device_id=(src_peer(d), t), device_id_type=MESH)
    pl.semaphore_wait(barrier, n_snk + n_src - 2)

    def cast(piece, kind, q, target):
        return pltpu.make_async_remote_copy(
            src_ref=right_buf.at[piece], dst_ref=right_buf.at[piece],
            send_sem=cast_send.at[kind, q], recv_sem=cast_recv.at[piece],
            device_id=(s, target), device_id_type=MESH,
        )

    def cast_ways(q):
        mine = low * half + q
        return (
            (goes_up, cast(mine, 0, q, jnp.minimum(t + 2, n_snk - 1))),
            (goes_down, cast(mine, 1, q, jnp.maximum(t - 2, 0))),
            (jnp.logical_not(pair_is_root), cast(mine, 2, q, high * 2 + other)),
        )

    def cast_rest(q):
        return cast(other * half + q, 3, q, high * 2 + other)

    def cast_arrived(piece):
        cast(piece, 0, 0, high * 2 + other).wait_recv()

    @pl.when(is_root)
    def _():
        for block in range(2 * mom):
            for r in range(SPLIT):
                right_buf[block * SPLIT + r] = blocks_ref[block, r * cut : (r + 1) * cut]

        def send(q, carry):
            cast_rest(q).start()
            for taken, copy in cast_ways(q):
                pl.when(taken)(copy.start)
            return carry

        lax.fori_loop(0, half, send, 0)

    tau_copies = []
    for d in range(1, n_snk):
        copy = pltpu.make_async_remote_copy(
            src_ref=tau_ref.at[snk_peer(d)], dst_ref=tau_in.at[t],
            send_sem=tau_send.at[d - 1], recv_sem=tau_recv.at[d - 1],
            device_id=(s, snk_peer(d)), device_id_type=MESH,
        )
        copy.start()
        tau_copies.append(copy)
    tau_in[t] = tau_ref[t]

    table_row = lax.broadcasted_iota(jnp.int32, (NW, 1), 0)
    picks = table_row == weight_ref[...]
    slot = (node_ref[...] * mom + right_ref[...]) * mom + left_ref[...]
    slots = NODES * mom * mom
    feeds = lax.broadcasted_iota(jnp.int32, (slots, 1), 0) == slot
    for c in range(2):
        gain = jnp.sum(jnp.where(picks, table_ref[:, c : c + 1], 0.0), axis=0, keepdims=True)
        total = jnp.sum(jnp.where(feeds, gain, 0.0), axis=1, keepdims=True)
        coef[c] = jnp.broadcast_to(total, (slots, order))

    def mix_node(n, first, last):
        def step(i, carry):
            span = pl.ds(pl.multiple_of(i * MIX_ROWS, MIX_ROWS), MIX_ROWS)
            real = [blocks_ref[2 * a, span, :].astype(F32) for a in range(mom)]
            imag = [blocks_ref[2 * a + 1, span, :].astype(F32) for a in range(mom)]
            for b in range(mom):
                sum_real = sum_imag = 0.0
                for a in range(mom):
                    k = (n * mom + b) * mom + a
                    gain_real, gain_imag = coef[0, k : k + 1, :], coef[1, k : k + 1, :]
                    sum_real += gain_real * real[a] - gain_imag * imag[a]
                    sum_imag += gain_real * imag[a] + gain_imag * real[a]
                at = 2 * b * order
                mixed[n, span, at : at + order] = sum_real.astype(BF16)
                mixed[n, span, at + order : at + 2 * order] = sum_imag.astype(BF16)
            return carry

        lax.fori_loop(first, last, step, 0)

    turns = half // NODES
    mix_steps = order // MIX_ROWS // turns
    with jax.named_scope("relay_and_mix"):
        for n in range(NODES):

            def relay(j, carry):
                q = n * turns + j

                @pl.when(jnp.logical_not(is_root))
                def _():
                    cast_arrived(low * half + q)
                    for taken, copy in cast_ways(q):
                        pl.when(taken)(copy.start)

                mix_node(n, j * mix_steps, (j + 1) * mix_steps)
                return carry

            lax.fori_loop(0, turns, relay, 0)

    with jax.named_scope("tau"):
        for copy in tau_copies:
            copy.wait_recv()
        whole = tau_in[...].astype(F32)
        tau_real = whole[:, 0].reshape(order, order).T
        tau_imag = whole[:, 1].reshape(order, order).T
        tau_cat[:order, :order] = tau_real.astype(BF16)
        tau_cat[:order, order:] = (-tau_imag).astype(BF16)
        tau_cat[order:, :order] = tau_imag.astype(BF16)
        tau_cat[order:, order:] = tau_real.astype(BF16)

    with jax.named_scope("times_right"):
        for j in range(mom):
            if 2 * j < mom:
                b = low * (mom // 2) + j
            else:
                b = other * (mom // 2) + j - mom // 2
                @pl.when(jnp.logical_not(is_root))
                def _():
                    for r in range(2 * SPLIT):
                        cast_arrived(2 * b * SPLIT + r)

            right = right_buf[pl.ds(2 * b * SPLIT, 2 * SPLIT)].reshape(2 * order, order)
            both = jnp.dot(tau_cat[...], right, preferred_element_type=F32)
            prod[0, b, :order] = both[:order].astype(BF16)
            prod[0, b, order:] = (-both[order:]).astype(BF16)
            prod[1, b, :order] = both[order:].astype(BF16)
            prod[1, b, order:] = both[:order].astype(BF16)

    def plane_of(p):
        return jnp.dot(
            mixed[p // 2], prod[p % 2].reshape(2 * mom * order, order), preferred_element_type=F32
        )

    part_copies = []
    with jax.named_scope("nodes"):
        for d in range(1, n_src):
            for q in range(planes):
                part[d - 1, q] = plane_of(src_peer(d) * planes + q).astype(BF16)
            copy = pltpu.make_async_remote_copy(
                src_ref=part.at[d - 1], dst_ref=part_in.at[d - 1],
                send_sem=part_send.at[d - 1], recv_sem=part_recv.at[d - 1],
                device_id=(src_peer(d), t), device_id_type=MESH,
            )
            copy.start()
            part_copies.append(copy)
        own = [plane_of(s * planes + q) for q in range(planes)]

    with jax.named_scope("sum_src"):
        for copy in part_copies:
            copy.wait_recv()
        for q in range(planes):
            total = own[q]
            for d in range(1, n_src):
                total += part_in[d - 1, q].astype(F32)
            for k in range(n_snk):
                share[k, q] = total[k * rows : (k + 1) * rows].astype(BF16)

    with jax.named_scope("sum_snk"):
        share_copies = []
        for d in range(1, n_snk):
            copy = pltpu.make_async_remote_copy(
                src_ref=share.at[snk_peer(d)], dst_ref=share_in.at[d - 1],
                send_sem=share_send.at[d - 1], recv_sem=share_recv.at[d - 1],
                device_id=(s, snk_peer(d)), device_id_type=MESH,
            )
            copy.start()
            share_copies.append(copy)
        total = share[t].astype(F32)
        for d in range(1, n_snk):
            share_copies[d - 1].wait_recv()
            total += share_in[d - 1].astype(F32)
        done[s] = total.astype(BF16)

    with jax.named_scope("spread"):
        done_copies = []
        for d in range(1, n_src):
            copy = pltpu.make_async_remote_copy(
                src_ref=done.at[s], dst_ref=done.at[s],
                send_sem=done_send.at[d - 1], recv_sem=done_recv.at[d - 1],
                device_id=(src_peer(d), t), device_id_type=MESH,
            )
            copy.start()
            done_copies.append(copy)
        for copy in done_copies:
            copy.wait_recv()
        out_ref[...] = done[...]

    def sent(q, carry):
        for taken, copy in cast_ways(q):
            pl.when(taken)(copy.wait_send)
        pl.when(is_root)(cast_rest(q).wait_send)
        return carry

    lax.fori_loop(0, half, sent, 0)
    for copy in tau_copies + part_copies + share_copies + done_copies:
        copy.wait_send()


def shards(peram, meson_blocks, edge_left, edge_right, edge_node, edge_weight, weight_table):
    n_src, n_snk = lax.axis_size("src"), lax.axis_size("snk")
    mom, order = meson_blocks.shape[1], meson_blocks.shape[3]
    rows, planes = order // n_snk, NODES * 2 // n_src
    tau = jnp.swapaxes(peram[0], 2, 3)
    blocks = meson_blocks.reshape(2 * mom, order, order)
    edges = [e.reshape(1, -1) for e in (edge_left, edge_right, edge_node, edge_weight)]
    dma = pltpu.SemaphoreType.DMA
    out = pl.pallas_call(
        functools.partial(kernel, n_src, n_snk, mom, order),
        out_shape=jax.ShapeDtypeStruct((n_src, planes, rows, order), BF16),
        in_specs=[pl.BlockSpec(memory_space=pltpu.VMEM)] * 7,
        out_specs=pl.BlockSpec(memory_space=pltpu.VMEM),
        scratch_shapes=[
            pltpu.VMEM((n_snk, 2, rows, order), BF16),
            pltpu.VMEM((2 * mom * SPLIT, order // SPLIT, order), BF16),
            pltpu.VMEM((2, NODES * mom * mom, order), F32),
            pltpu.VMEM((NODES, order, 2 * mom * order), BF16),
            pltpu.VMEM((2 * order, 2 * order), BF16),
            pltpu.VMEM((2, mom, 2 * order, order), BF16),
            pltpu.VMEM((n_src - 1, planes, order, order), BF16),
            pltpu.VMEM((n_src - 1, planes, order, order), BF16),
            pltpu.VMEM((n_snk, planes, rows, order), BF16),
            pltpu.VMEM((n_snk - 1, planes, rows, order), BF16),
            pltpu.VMEM((n_src, planes, rows, order), BF16),
            dma((n_snk - 1,)), dma((n_snk - 1,)),
            dma((4, mom * SPLIT)), dma((2 * mom * SPLIT,)),
            dma((n_src - 1,)), dma((n_src - 1,)),
            dma((n_snk - 1,)), dma((n_snk - 1,)),
            dma((n_src - 1,)), dma((n_src - 1,)),
        ],
        compiler_params=pltpu.CompilerParams(
            collective_id=0, has_side_effects=True, vmem_limit_bytes=40 * 2**20
        ),
    )(tau, blocks, *edges, weight_table)
    out = out.reshape(NODES, 2, rows, order)
    return jnp.transpose(out, (2, 0, 1, 3))


def solution(mesh):
    return jax.shard_map(
        shards,
        mesh=mesh,
        in_specs=(
            P("src", None, None, None, "snk"),
            P("snk", None, None, None, None),
            P("src", "snk", None),
            P("src", "snk", None),
            P("src", "snk", None),
            P("src", "snk", None),
            P(),
        ),
        out_specs=P("snk", None, None, None),
        check_vma=False,
    )
```

```python
import functools

import jax
import jax.numpy as jnp
from jax import lax
from jax.experimental import pallas as pl
from jax.experimental.pallas import tpu as pltpu
from jax.sharding import PartitionSpec as P

NODES = 4
NW = 16
MESH = pl.DeviceIdType.MESH
F32 = jnp.float32
BF16 = jnp.bfloat16
MIX_ROWS = 16


def kernel(
    n_src, n_snk, mom, order,
    tau_ref, blocks_hbm, left_ref, right_ref, node_ref, weight_ref, table_ref,
    out_ref,
    blocks_ref, tau_in, right_buf, coef, mixed, tau_cat, prod, part, part_in, share, share_in, done,
    tau_send, tau_recv, cast_send, cast_recv, part_send, part_recv, share_send, share_recv, done_send, done_recv, local_sem,
):
    s = lax.axis_index("src")
    t = lax.axis_index("snk")
    planes = NODES * 2 // n_src
    rows = order // n_snk
    half = mom
    root = s * (n_snk // n_src)
    high, low = t // 2, t % 2
    root_high, root_low = root // 2, root % 2
    other = 1 - low
    is_root = t == root
    pair_is_root = (high == root_high) & (other == root_low)
    goes_up = (high >= root_high) & (high + 1 < n_snk // 2)
    goes_down = (high <= root_high) & (high >= 1)

    def snk_peer(d):
        return lax.rem(t + d, n_snk)

    def src_peer(d):
        return lax.rem(s + d, n_src)

    load_blocks = pltpu.make_async_copy(blocks_hbm, blocks_ref, local_sem.at[0])
    load_tau = pltpu.make_async_copy(tau_ref.at[t], tau_in.at[t], local_sem.at[1])
    load_right = pltpu.make_async_copy(blocks_hbm, right_buf, local_sem.at[2])
    pl.when(is_root)(load_right.start)
    load_blocks.start()
    load_tau.start()

    barrier = pltpu.get_barrier_semaphore()
    for d in range(1, n_snk):
        pl.semaphore_signal(barrier, inc=1, device_id=(s, snk_peer(d)), device_id_type=MESH)
    for d in range(1, n_src):
        pl.semaphore_signal(barrier, inc=1, device_id=(src_peer(d), t), device_id_type=MESH)
    pl.semaphore_wait(barrier, n_snk + n_src - 2)

    def cast(piece, kind, q, target):
        return pltpu.make_async_remote_copy(
            src_ref=right_buf.at[piece], dst_ref=right_buf.at[piece],
            send_sem=cast_send.at[kind, q], recv_sem=cast_recv.at[piece],
            device_id=(s, target), device_id_type=MESH,
        )

    def cast_ways(q):
        mine = low * half + q
        return (
            (goes_up, cast(mine, 0, q, jnp.minimum(t + 2, n_snk - 1))),
            (goes_down, cast(mine, 1, q, jnp.maximum(t - 2, 0))),
            (jnp.logical_not(pair_is_root), cast(mine, 2, q, high * 2 + other)),
        )

    def cast_rest(q):
        return cast(other * half + q, 3, q, high * 2 + other)

    def cast_arrived(piece):
        @pl.when(jnp.logical_not(is_root))
        def _():
            cast(piece, 0, 0, high * 2 + other).wait_recv()

    @pl.when(is_root)
    def _():
        load_right.wait()
        for q in range(half):
            cast_rest(q).start()

    tau_copies = []
    for d in range(1, n_snk):
        copy = pltpu.make_async_remote_copy(
            src_ref=tau_ref.at[snk_peer(d)], dst_ref=tau_in.at[t],
            send_sem=tau_send.at[d - 1], recv_sem=tau_recv.at[d - 1],
            device_id=(s, snk_peer(d)), device_id_type=MESH,
        )
        copy.start()
        tau_copies.append(copy)

    table_row = lax.broadcasted_iota(jnp.int32, (NW, 1), 0)
    picks = table_row == weight_ref[...]
    slot = (node_ref[...] * mom + right_ref[...]) * mom + left_ref[...]
    slots = NODES * mom * mom
    feeds = lax.broadcasted_iota(jnp.int32, (slots, 1), 0) == slot
    for c in range(2):
        gain = jnp.sum(jnp.where(picks, table_ref[:, c : c + 1], 0.0), axis=0, keepdims=True)
        total = jnp.sum(jnp.where(feeds, gain, 0.0), axis=1, keepdims=True)
        coef[c] = jnp.broadcast_to(total, (slots, order))

    def mix_node(n):
        def step(i, carry):
            span = pl.ds(pl.multiple_of(i * MIX_ROWS, MIX_ROWS), MIX_ROWS)
            real = [blocks_ref[2 * a, span, :].astype(F32) for a in range(mom)]
            imag = [blocks_ref[2 * a + 1, span, :].astype(F32) for a in range(mom)]
            for b in range(mom):
                sum_real = sum_imag = 0.0
                for a in range(mom):
                    k = (n * mom + b) * mom + a
                    gain_real, gain_imag = coef[0, k : k + 1, :], coef[1, k : k + 1, :]
                    sum_real += gain_real * real[a] - gain_imag * imag[a]
                    sum_imag += gain_real * imag[a] + gain_imag * real[a]
                at = 2 * b * order
                mixed[n, span, at : at + order] = sum_real.astype(BF16)
                mixed[n, span, at + order : at + 2 * order] = sum_imag.astype(BF16)
            return carry

        lax.fori_loop(0, order // MIX_ROWS, step, 0)

    load_blocks.wait()
    with jax.named_scope("relay_and_mix"):
        for q in range(max(half, NODES)):
            if q < half:
                cast_arrived(low * half + q)
                for taken, copy in cast_ways(q):
                    pl.when(taken)(copy.start)
            if q < NODES:
                mix_node(q)

    with jax.named_scope("tau"):
        for copy in tau_copies:
            copy.wait_recv()
        load_tau.wait()
        whole = tau_in[...].astype(F32)
        tau_real = whole[:, 0].reshape(order, order).T
        tau_imag = whole[:, 1].reshape(order, order).T
        tau_cat[:order, :order] = tau_real.astype(BF16)
        tau_cat[:order, order:] = (-tau_imag).astype(BF16)
        tau_cat[order:, :order] = tau_imag.astype(BF16)
        tau_cat[order:, order:] = tau_real.astype(BF16)

    with jax.named_scope("times_right"):
        for j in range(mom):
            if 2 * j < mom:
                b = low * (mom // 2) + j
            else:
                b = other * (mom // 2) + j - mom // 2
                cast_arrived(2 * b)
                cast_arrived(2 * b + 1)
            right = right_buf[pl.ds(2 * b, 2)].reshape(2 * order, order)
            both = jnp.dot(tau_cat[...], right, preferred_element_type=F32)
            prod[0, b, :order] = both[:order].astype(BF16)
            prod[0, b, order:] = (-both[order:]).astype(BF16)
            prod[1, b, :order] = both[order:].astype(BF16)
            prod[1, b, order:] = both[:order].astype(BF16)

    def plane_of(p):
        return jnp.dot(
            mixed[p // 2], prod[p % 2].reshape(2 * mom * order, order), preferred_element_type=F32
        )

    part_copies = []
    with jax.named_scope("nodes"):
        for d in range(1, n_src):
            for q in range(planes):
                part[d - 1, q] = plane_of(src_peer(d) * planes + q).astype(BF16)
            copy = pltpu.make_async_remote_copy(
                src_ref=part.at[d - 1], dst_ref=part_in.at[d - 1],
                send_sem=part_send.at[d - 1], recv_sem=part_recv.at[d - 1],
                device_id=(src_peer(d), t), device_id_type=MESH,
            )
            copy.start()
            part_copies.append(copy)
        own = [plane_of(s * planes + q) for q in range(planes)]

    with jax.named_scope("sum_src"):
        for copy in part_copies:
            copy.wait_recv()
        for q in range(planes):
            total = own[q]
            for d in range(1, n_src):
                total += part_in[d - 1, q].astype(F32)
            for k in range(n_snk):
                share[k, q] = total[k * rows : (k + 1) * rows].astype(BF16)

    with jax.named_scope("sum_snk"):
        share_copies = []
        for d in range(1, n_snk):
            copy = pltpu.make_async_remote_copy(
                src_ref=share.at[snk_peer(d)], dst_ref=share_in.at[d - 1],
                send_sem=share_send.at[d - 1], recv_sem=share_recv.at[d - 1],
                device_id=(s, snk_peer(d)), device_id_type=MESH,
            )
            copy.start()
            share_copies.append(copy)
        total = share[t].astype(F32)
        for d in range(1, n_snk):
            share_copies[d - 1].wait_recv()
            total += share_in[d - 1].astype(F32)
        done[s] = total.astype(BF16)

    with jax.named_scope("spread"):
        done_copies = []
        for d in range(1, n_src):
            copy = pltpu.make_async_remote_copy(
                src_ref=done.at[s], dst_ref=done.at[s],
                send_sem=done_send.at[d - 1], recv_sem=done_recv.at[d - 1],
                device_id=(src_peer(d), t), device_id_type=MESH,
            )
            copy.start()
            done_copies.append(copy)
        for copy in done_copies:
            copy.wait_recv()
        out_ref[...] = done[...]

    for q in range(half):
        for taken, copy in cast_ways(q):
            pl.when(taken)(copy.wait_send)
        pl.when(is_root)(cast_rest(q).wait_send)
    for copy in tau_copies + part_copies + share_copies + done_copies:
        copy.wait_send()


def shards(peram, meson_blocks, edge_left, edge_right, edge_node, edge_weight, weight_table):
    n_src, n_snk = lax.axis_size("src"), lax.axis_size("snk")
    mom, order = meson_blocks.shape[1], meson_blocks.shape[3]
    rows, planes = order // n_snk, NODES * 2 // n_src
    tau = jnp.swapaxes(peram[0], 2, 3)
    blocks = meson_blocks.reshape(2 * mom, order, order)
    edges = [e.reshape(1, -1) for e in (edge_left, edge_right, edge_node, edge_weight)]
    dma = pltpu.SemaphoreType.DMA
    out = pl.pallas_call(
        functools.partial(kernel, n_src, n_snk, mom, order),
        out_shape=jax.ShapeDtypeStruct((n_src, planes, rows, order), BF16),
        in_specs=[pl.BlockSpec(memory_space=pltpu.HBM)] * 2
        + [pl.BlockSpec(memory_space=pltpu.VMEM)] * 5,
        out_specs=pl.BlockSpec(memory_space=pltpu.VMEM),
        scratch_shapes=[
            pltpu.VMEM((2 * mom, order, order), BF16),
            pltpu.VMEM((n_snk, 2, rows, order), BF16),
            pltpu.VMEM((2 * mom, order, order), BF16),
            pltpu.VMEM((2, NODES * mom * mom, order), F32),
            pltpu.VMEM((NODES, order, 2 * mom * order), BF16),
            pltpu.VMEM((2 * order, 2 * order), BF16),
            pltpu.VMEM((2, mom, 2 * order, order), BF16),
            pltpu.VMEM((n_src - 1, planes, order, order), BF16),
            pltpu.VMEM((n_src - 1, planes, order, order), BF16),
            pltpu.VMEM((n_snk, planes, rows, order), BF16),
            pltpu.VMEM((n_snk - 1, planes, rows, order), BF16),
            pltpu.VMEM((n_src, planes, rows, order), BF16),
            dma((n_snk - 1,)), dma((n_snk - 1,)),
            dma((4, mom)), dma((2 * mom,)),
            dma((n_src - 1,)), dma((n_src - 1,)),
            dma((n_snk - 1,)), dma((n_snk - 1,)),
            dma((n_src - 1,)), dma((n_src - 1,)),
            dma((3,)),
        ],
        compiler_params=pltpu.CompilerParams(
            collective_id=0, has_side_effects=True, vmem_limit_bytes=40 * 2**20
        ),
    )(tau, blocks, *edges, weight_table)
    out = out.reshape(NODES, 2, rows, order)
    return jnp.transpose(out, (2, 0, 1, 3))


def solution(mesh):
    return jax.shard_map(
        shards,
        mesh=mesh,
        in_specs=(
            P("src", None, None, None, "snk"),
            P("snk", None, None, None, None),
            P("src", "snk", None),
            P("src", "snk", None),
            P("src", "snk", None),
            P("src", "snk", None),
            P(),
        ),
        out_specs=P("snk", None, None, None),
        check_vma=False,
    )
```

```python
import functools

import jax
import jax.numpy as jnp
from jax import lax
from jax.experimental import pallas as pl
from jax.experimental.pallas import tpu as pltpu
from jax.sharding import PartitionSpec as P

NODES = 4
NW = 16
MESH = pl.DeviceIdType.MESH
F32 = jnp.float32
BF16 = jnp.bfloat16
MIX_ROWS = 16


def kernel(
    n_src, n_snk, mom, order,
    tau_ref, blocks_ref, left_ref, right_ref, node_ref, weight_ref, table_ref,
    out_ref,
    tau_in, right_buf, coef, mixed, tau_cat, prod, part, part_in, share, share_in, done,
    tau_send, tau_recv, cast_send, cast_recv, part_send, part_recv, share_send, share_recv, done_send, done_recv,
):
    s = lax.axis_index("src")
    t = lax.axis_index("snk")
    planes = NODES * 2 // n_src
    rows = order // n_snk
    half = mom
    root = s * (n_snk // n_src)
    high, low = t // 2, t % 2
    root_high, root_low = root // 2, root % 2
    other = 1 - low
    is_root = t == root
    pair_is_root = (high == root_high) & (other == root_low)
    goes_up = (high >= root_high) & (high + 1 < n_snk // 2)
    goes_down = (high <= root_high) & (high >= 1)

    def snk_peer(d):
        return lax.rem(t + d, n_snk)

    def src_peer(d):
        return lax.rem(s + d, n_src)

    barrier = pltpu.get_barrier_semaphore()
    for d in range(1, n_snk):
        pl.semaphore_signal(barrier, inc=1, device_id=(s, snk_peer(d)), device_id_type=MESH)
    for d in range(1, n_src):
        pl.semaphore_signal(barrier, inc=1, device_id=(src_peer(d), t), device_id_type=MESH)
    pl.semaphore_wait(barrier, n_snk + n_src - 2)

    def cast(piece, kind, q, target):
        return pltpu.make_async_remote_copy(
            src_ref=right_buf.at[piece], dst_ref=right_buf.at[piece],
            send_sem=cast_send.at[kind, q], recv_sem=cast_recv.at[piece],
            device_id=(s, target), device_id_type=MESH,
        )

    def cast_ways(q):
        mine = low * half + q
        return (
            (goes_up, cast(mine, 0, q, jnp.minimum(t + 2, n_snk - 1))),
            (goes_down, cast(mine, 1, q, jnp.maximum(t - 2, 0))),
            (jnp.logical_not(pair_is_root), cast(mine, 2, q, high * 2 + other)),
        )

    def cast_rest(q):
        return cast(other * half + q, 3, q, high * 2 + other)

    def cast_arrived(piece):
        @pl.when(jnp.logical_not(is_root))
        def _():
            cast(piece, 0, 0, high * 2 + other).wait_recv()

    @pl.when(is_root)
    def _():
        for piece in range(2 * mom):
            right_buf[piece] = blocks_ref[piece]
        for q in range(half):
            for taken, copy in cast_ways(q)[:2]:
                pl.when(taken)(copy.start)
            cast_rest(q).start()
        for q in range(half):
            cast_ways(q)[2][1].start()

    tau_copies = []
    for d in range(1, n_snk):
        copy = pltpu.make_async_remote_copy(
            src_ref=tau_ref.at[snk_peer(d)], dst_ref=tau_in.at[t],
            send_sem=tau_send.at[d - 1], recv_sem=tau_recv.at[d - 1],
            device_id=(s, snk_peer(d)), device_id_type=MESH,
        )
        copy.start()
        tau_copies.append(copy)
    tau_in[t] = tau_ref[t]

    table_row = lax.broadcasted_iota(jnp.int32, (NW, 1), 0)
    picks = table_row == weight_ref[...]
    slot = (node_ref[...] * mom + right_ref[...]) * mom + left_ref[...]
    slots = NODES * mom * mom
    feeds = lax.broadcasted_iota(jnp.int32, (slots, 1), 0) == slot
    for c in range(2):
        gain = jnp.sum(jnp.where(picks, table_ref[:, c : c + 1], 0.0), axis=0, keepdims=True)
        total = jnp.sum(jnp.where(feeds, gain, 0.0), axis=1, keepdims=True)
        coef[c] = jnp.broadcast_to(total, (slots, order))

    def mix_node(n):
        def step(i, carry):
            span = pl.ds(pl.multiple_of(i * MIX_ROWS, MIX_ROWS), MIX_ROWS)
            real = [blocks_ref[2 * a, span, :].astype(F32) for a in range(mom)]
            imag = [blocks_ref[2 * a + 1, span, :].astype(F32) for a in range(mom)]
            for b in range(mom):
                sum_real = sum_imag = 0.0
                for a in range(mom):
                    k = (n * mom + b) * mom + a
                    gain_real, gain_imag = coef[0, k : k + 1, :], coef[1, k : k + 1, :]
                    sum_real += gain_real * real[a] - gain_imag * imag[a]
                    sum_imag += gain_real * imag[a] + gain_imag * real[a]
                at = 2 * b * order
                mixed[n, span, at : at + order] = sum_real.astype(BF16)
                mixed[n, span, at + order : at + 2 * order] = sum_imag.astype(BF16)
            return carry

        lax.fori_loop(0, order // MIX_ROWS, step, 0)

    with jax.named_scope("relay_and_mix"):
        for q in range(max(half, NODES)):
            if q < half:
                cast_arrived(low * half + q)
                for taken, copy in cast_ways(q):
                    pl.when(taken & jnp.logical_not(is_root))(copy.start)
            if q < NODES:
                mix_node(q)

    with jax.named_scope("tau"):
        for copy in tau_copies:
            copy.wait_recv()
        whole = tau_in[...].astype(F32)
        tau_real = whole[:, 0].reshape(order, order).T
        tau_imag = whole[:, 1].reshape(order, order).T
        tau_cat[:order, :order] = tau_real.astype(BF16)
        tau_cat[:order, order:] = (-tau_imag).astype(BF16)
        tau_cat[order:, :order] = tau_imag.astype(BF16)
        tau_cat[order:, order:] = tau_real.astype(BF16)

    with jax.named_scope("times_right"):
        for j in range(mom):
            if 2 * j < mom:
                b = low * (mom // 2) + j
            else:
                b = other * (mom // 2) + j - mom // 2
                cast_arrived(2 * b)
                cast_arrived(2 * b + 1)
            right = right_buf[pl.ds(2 * b, 2)].reshape(2 * order, order)
            both = jnp.dot(tau_cat[...], right, preferred_element_type=F32)
            prod[0, b, :order] = both[:order].astype(BF16)
            prod[0, b, order:] = (-both[order:]).astype(BF16)
            prod[1, b, :order] = both[order:].astype(BF16)
            prod[1, b, order:] = both[:order].astype(BF16)

    def plane_of(p):
        return jnp.dot(
            mixed[p // 2], prod[p % 2].reshape(2 * mom * order, order), preferred_element_type=F32
        )

    part_copies = []
    with jax.named_scope("nodes"):
        for d in range(1, n_src):
            for q in range(planes):
                part[d - 1, q] = plane_of(src_peer(d) * planes + q).astype(BF16)
            copy = pltpu.make_async_remote_copy(
                src_ref=part.at[d - 1], dst_ref=part_in.at[d - 1],
                send_sem=part_send.at[d - 1], recv_sem=part_recv.at[d - 1],
                device_id=(src_peer(d), t), device_id_type=MESH,
            )
            copy.start()
            part_copies.append(copy)
        own = [plane_of(s * planes + q) for q in range(planes)]

    with jax.named_scope("sum_src"):
        for copy in part_copies:
            copy.wait_recv()
        for q in range(planes):
            total = own[q]
            for d in range(1, n_src):
                total += part_in[d - 1, q].astype(F32)
            for k in range(n_snk):
                share[k, q] = total[k * rows : (k + 1) * rows].astype(BF16)

    with jax.named_scope("sum_snk"):
        share_copies = []
        for d in range(1, n_snk):
            copy = pltpu.make_async_remote_copy(
                src_ref=share.at[snk_peer(d)], dst_ref=share_in.at[d - 1],
                send_sem=share_send.at[d - 1], recv_sem=share_recv.at[d - 1],
                device_id=(s, snk_peer(d)), device_id_type=MESH,
            )
            copy.start()
            share_copies.append(copy)
        total = share[t].astype(F32)
        for d in range(1, n_snk):
            share_copies[d - 1].wait_recv()
            total += share_in[d - 1].astype(F32)
        done[s] = total.astype(BF16)

    with jax.named_scope("spread"):
        done_copies = []
        for d in range(1, n_src):
            copy = pltpu.make_async_remote_copy(
                src_ref=done.at[s], dst_ref=done.at[s],
                send_sem=done_send.at[d - 1], recv_sem=done_recv.at[d - 1],
                device_id=(src_peer(d), t), device_id_type=MESH,
            )
            copy.start()
            done_copies.append(copy)
        for copy in done_copies:
            copy.wait_recv()
        out_ref[...] = done[...]

    for q in range(half):
        for taken, copy in cast_ways(q):
            pl.when(taken)(copy.wait_send)
        pl.when(is_root)(cast_rest(q).wait_send)
    for copy in tau_copies + part_copies + share_copies + done_copies:
        copy.wait_send()


def shards(peram, meson_blocks, edge_left, edge_right, edge_node, edge_weight, weight_table):
    n_src, n_snk = lax.axis_size("src"), lax.axis_size("snk")
    mom, order = meson_blocks.shape[1], meson_blocks.shape[3]
    rows, planes = order // n_snk, NODES * 2 // n_src
    tau = jnp.swapaxes(peram[0], 2, 3)
    blocks = meson_blocks.reshape(2 * mom, order, order)
    edges = [e.reshape(1, -1) for e in (edge_left, edge_right, edge_node, edge_weight)]
    dma = pltpu.SemaphoreType.DMA
    out = pl.pallas_call(
        functools.partial(kernel, n_src, n_snk, mom, order),
        out_shape=jax.ShapeDtypeStruct((n_src, planes, rows, order), BF16),
        in_specs=[pl.BlockSpec(memory_space=pltpu.VMEM)] * 7,
        out_specs=pl.BlockSpec(memory_space=pltpu.VMEM),
        scratch_shapes=[
            pltpu.VMEM((n_snk, 2, rows, order), BF16),
            pltpu.VMEM((2 * mom, order, order), BF16),
            pltpu.VMEM((2, NODES * mom * mom, order), F32),
            pltpu.VMEM((NODES, order, 2 * mom * order), BF16),
            pltpu.VMEM((2 * order, 2 * order), BF16),
            pltpu.VMEM((2, mom, 2 * order, order), BF16),
            pltpu.VMEM((n_src - 1, planes, order, order), BF16),
            pltpu.VMEM((n_src - 1, planes, order, order), BF16),
            pltpu.VMEM((n_snk, planes, rows, order), BF16),
            pltpu.VMEM((n_snk - 1, planes, rows, order), BF16),
            pltpu.VMEM((n_src, planes, rows, order), BF16),
            dma((n_snk - 1,)), dma((n_snk - 1,)),
            dma((4, mom)), dma((2 * mom,)),
            dma((n_src - 1,)), dma((n_src - 1,)),
            dma((n_snk - 1,)), dma((n_snk - 1,)),
            dma((n_src - 1,)), dma((n_src - 1,)),
        ],
        compiler_params=pltpu.CompilerParams(
            collective_id=0, has_side_effects=True, vmem_limit_bytes=40 * 2**20
        ),
    )(tau, blocks, *edges, weight_table)
    out = out.reshape(NODES, 2, rows, order)
    return jnp.transpose(out, (2, 0, 1, 3))


def solution(mesh):
    return jax.shard_map(
        shards,
        mesh=mesh,
        in_specs=(
            P("src", None, None, None, "snk"),
            P("snk", None, None, None, None),
            P("src", "snk", None),
            P("src", "snk", None),
            P("src", "snk", None),
            P("src", "snk", None),
            P(),
        ),
        out_specs=P("snk", None, None, None),
        check_vma=False,
    )
```

```python
import functools

import jax
import jax.numpy as jnp
from jax import lax
from jax.experimental import pallas as pl
from jax.experimental.pallas import tpu as pltpu
from jax.sharding import PartitionSpec as P

NODES = 4
NW = 16
MESH = pl.DeviceIdType.MESH
F32 = jnp.float32
BF16 = jnp.bfloat16
MIX_ROWS = 16


def kernel(
    n_src, n_snk, mom, order,
    tau_ref, blocks_ref, left_ref, right_ref, node_ref, weight_ref, table_ref,
    out_ref,
    tau_in, right_buf, coef, mixed, tau_cat, prod, part, part_in, share, share_in, done,
    tau_send, tau_recv, cast_send, cast_recv, part_send, part_recv, share_send, share_recv, done_send, done_recv,
):
    s = lax.axis_index("src")
    t = lax.axis_index("snk")
    planes = NODES * 2 // n_src
    rows = order // n_snk
    half = mom
    root = s * (n_snk // n_src)
    high, low = t // 2, t % 2
    root_high, root_low = root // 2, root % 2
    other = 1 - low
    is_root = t == root
    pair_is_root = (high == root_high) & (other == root_low)
    goes_up = (high >= root_high) & (high + 1 < n_snk // 2)
    goes_down = (high <= root_high) & (high >= 1)

    assist = lax.rem(s + n_src // 2, n_src)
    assist_root = assist * (n_snk // n_src)
    assist_low = assist_root % 2
    assist_pair = assist_root + 1 - 2 * assist_low
    is_helper = t == assist_root
    is_pair = (high == root_high) & (low != root_low)
    own_pair = half // 2

    def snk_peer(d):
        return lax.rem(t + d, n_snk)

    def src_peer(d):
        return lax.rem(s + d, n_src)

    barrier = pltpu.get_barrier_semaphore()
    for d in range(1, n_snk):
        pl.semaphore_signal(barrier, inc=1, device_id=(s, snk_peer(d)), device_id_type=MESH)
    for d in range(1, n_src):
        pl.semaphore_signal(barrier, inc=1, device_id=(src_peer(d), t), device_id_type=MESH)

    @pl.when(is_pair)
    def _():
        pl.semaphore_signal(barrier, inc=1, device_id=(assist, root), device_id_type=MESH)

    pl.semaphore_wait(barrier, n_snk + n_src - 2 + is_helper.astype(jnp.int32))

    def help_pair(q):
        piece = assist_low * half + q
        return pltpu.make_async_remote_copy(
            src_ref=blocks_ref.at[piece], dst_ref=right_buf.at[piece],
            send_sem=cast_send.at[4, q], recv_sem=cast_recv.at[piece],
            device_id=(assist, assist_pair), device_id_type=MESH,
        )

    def cast(piece, kind, q, target):
        return pltpu.make_async_remote_copy(
            src_ref=right_buf.at[piece], dst_ref=right_buf.at[piece],
            send_sem=cast_send.at[kind, q], recv_sem=cast_recv.at[piece],
            device_id=(s, target), device_id_type=MESH,
        )

    def cast_ways(q):
        mine = low * half + q
        return (
            (goes_up, cast(mine, 0, q, jnp.minimum(t + 2, n_snk - 1))),
            (goes_down, cast(mine, 1, q, jnp.maximum(t - 2, 0))),
            (jnp.logical_not(pair_is_root) & (jnp.logical_not(is_root) | (q < own_pair)), cast(mine, 2, q, high * 2 + other)),
        )

    def cast_rest(q):
        return cast(other * half + q, 3, q, high * 2 + other)

    def cast_arrived(piece):
        @pl.when(jnp.logical_not(is_root))
        def _():
            cast(piece, 0, 0, high * 2 + other).wait_recv()

    @pl.when(is_root)
    def _():
        for piece in range(2 * mom):
            right_buf[piece] = blocks_ref[piece]
        for q in range(half):
            for taken, copy in cast_ways(q)[:2]:
                pl.when(taken)(copy.start)
            cast_rest(q).start()
        for q in range(own_pair):
            cast_ways(q)[2][1].start()

    @pl.when(is_helper)
    def _():
        for q in range(own_pair, half):
            help_pair(q).start()

    tau_copies = []
    for d in range(1, n_snk):
        copy = pltpu.make_async_remote_copy(
            src_ref=tau_ref.at[snk_peer(d)], dst_ref=tau_in.at[t],
            send_sem=tau_send.at[d - 1], recv_sem=tau_recv.at[d - 1],
            device_id=(s, snk_peer(d)), device_id_type=MESH,
        )
        copy.start()
        tau_copies.append(copy)
    tau_in[t] = tau_ref[t]

    table_row = lax.broadcasted_iota(jnp.int32, (NW, 1), 0)
    picks = table_row == weight_ref[...]
    slot = (node_ref[...] * mom + right_ref[...]) * mom + left_ref[...]
    slots = NODES * mom * mom
    feeds = lax.broadcasted_iota(jnp.int32, (slots, 1), 0) == slot
    for c in range(2):
        gain = jnp.sum(jnp.where(picks, table_ref[:, c : c + 1], 0.0), axis=0, keepdims=True)
        total = jnp.sum(jnp.where(feeds, gain, 0.0), axis=1, keepdims=True)
        coef[c] = jnp.broadcast_to(total, (slots, order))

    def mix_node(n):
        def step(i, carry):
            span = pl.ds(pl.multiple_of(i * MIX_ROWS, MIX_ROWS), MIX_ROWS)
            real = [blocks_ref[2 * a, span, :].astype(F32) for a in range(mom)]
            imag = [blocks_ref[2 * a + 1, span, :].astype(F32) for a in range(mom)]
            for b in range(mom):
                sum_real = sum_imag = 0.0
                for a in range(mom):
                    k = (n * mom + b) * mom + a
                    gain_real, gain_imag = coef[0, k : k + 1, :], coef[1, k : k + 1, :]
                    sum_real += gain_real * real[a] - gain_imag * imag[a]
                    sum_imag += gain_real * imag[a] + gain_imag * real[a]
                at = 2 * b * order
                mixed[n, span, at : at + order] = sum_real.astype(BF16)
                mixed[n, span, at + order : at + 2 * order] = sum_imag.astype(BF16)
            return carry

        lax.fori_loop(0, order // MIX_ROWS, step, 0)

    with jax.named_scope("relay_and_mix"):
        for q in range(max(half, NODES)):
            if q < half:
                cast_arrived(low * half + q)
                for taken, copy in cast_ways(q):
                    pl.when(taken & jnp.logical_not(is_root))(copy.start)
            if q < NODES:
                mix_node(q)

    with jax.named_scope("tau"):
        for copy in tau_copies:
            copy.wait_recv()
        whole = tau_in[...].astype(F32)
        tau_real = whole[:, 0].reshape(order, order).T
        tau_imag = whole[:, 1].reshape(order, order).T
        tau_cat[:order, :order] = tau_real.astype(BF16)
        tau_cat[:order, order:] = (-tau_imag).astype(BF16)
        tau_cat[order:, :order] = tau_imag.astype(BF16)
        tau_cat[order:, order:] = tau_real.astype(BF16)

    with jax.named_scope("times_right"):
        for j in range(mom):
            if 2 * j < mom:
                b = low * (mom // 2) + j
            else:
                b = other * (mom // 2) + j - mom // 2
                cast_arrived(2 * b)
                cast_arrived(2 * b + 1)
            right = right_buf[pl.ds(2 * b, 2)].reshape(2 * order, order)
            both = jnp.dot(tau_cat[...], right, preferred_element_type=F32)
            prod[0, b, :order] = both[:order].astype(BF16)
            prod[0, b, order:] = (-both[order:]).astype(BF16)
            prod[1, b, :order] = both[order:].astype(BF16)
            prod[1, b, order:] = both[:order].astype(BF16)

    def plane_of(p):
        return jnp.dot(
            mixed[p // 2], prod[p % 2].reshape(2 * mom * order, order), preferred_element_type=F32
        )

    part_copies = []
    with jax.named_scope("nodes"):
        for d in range(1, n_src):
            for q in range(planes):
                part[d - 1, q] = plane_of(src_peer(d) * planes + q).astype(BF16)
            copy = pltpu.make_async_remote_copy(
                src_ref=part.at[d - 1], dst_ref=part_in.at[d - 1],
                send_sem=part_send.at[d - 1], recv_sem=part_recv.at[d - 1],
                device_id=(src_peer(d), t), device_id_type=MESH,
            )
            copy.start()
            part_copies.append(copy)
        own = [plane_of(s * planes + q) for q in range(planes)]

    with jax.named_scope("sum_src"):
        for copy in part_copies:
            copy.wait_recv()
        for q in range(planes):
            total = own[q]
            for d in range(1, n_src):
                total += part_in[d - 1, q].astype(F32)
            for k in range(n_snk):
                share[k, q] = total[k * rows : (k + 1) * rows].astype(BF16)

    with jax.named_scope("sum_snk"):
        share_copies = []
        for d in range(1, n_snk):
            copy = pltpu.make_async_remote_copy(
                src_ref=share.at[snk_peer(d)], dst_ref=share_in.at[d - 1],
                send_sem=share_send.at[d - 1], recv_sem=share_recv.at[d - 1],
                device_id=(s, snk_peer(d)), device_id_type=MESH,
            )
            copy.start()
            share_copies.append(copy)
        total = share[t].astype(F32)
        for d in range(1, n_snk):
            share_copies[d - 1].wait_recv()
            total += share_in[d - 1].astype(F32)
        done[s] = total.astype(BF16)

    with jax.named_scope("spread"):
        done_copies = []
        for d in range(1, n_src):
            copy = pltpu.make_async_remote_copy(
                src_ref=done.at[s], dst_ref=done.at[s],
                send_sem=done_send.at[d - 1], recv_sem=done_recv.at[d - 1],
                device_id=(src_peer(d), t), device_id_type=MESH,
            )
            copy.start()
            done_copies.append(copy)
        for copy in done_copies:
            copy.wait_recv()
        out_ref[...] = done[...]

    for q in range(half):
        for taken, copy in cast_ways(q):
            pl.when(taken)(copy.wait_send)
        pl.when(is_root)(cast_rest(q).wait_send)
        if q >= own_pair:
            pl.when(is_helper)(help_pair(q).wait_send)
    for copy in tau_copies + part_copies + share_copies + done_copies:
        copy.wait_send()


def shards(peram, meson_blocks, edge_left, edge_right, edge_node, edge_weight, weight_table):
    n_src, n_snk = lax.axis_size("src"), lax.axis_size("snk")
    mom, order = meson_blocks.shape[1], meson_blocks.shape[3]
    rows, planes = order // n_snk, NODES * 2 // n_src
    tau = jnp.swapaxes(peram[0], 2, 3)
    blocks = meson_blocks.reshape(2 * mom, order, order)
    edges = [e.reshape(1, -1) for e in (edge_left, edge_right, edge_node, edge_weight)]
    dma = pltpu.SemaphoreType.DMA
    out = pl.pallas_call(
        functools.partial(kernel, n_src, n_snk, mom, order),
        out_shape=jax.ShapeDtypeStruct((n_src, planes, rows, order), BF16),
        in_specs=[pl.BlockSpec(memory_space=pltpu.VMEM)] * 7,
        out_specs=pl.BlockSpec(memory_space=pltpu.VMEM),
        scratch_shapes=[
            pltpu.VMEM((n_snk, 2, rows, order), BF16),
            pltpu.VMEM((2 * mom, order, order), BF16),
            pltpu.VMEM((2, NODES * mom * mom, order), F32),
            pltpu.VMEM((NODES, order, 2 * mom * order), BF16),
            pltpu.VMEM((2 * order, 2 * order), BF16),
            pltpu.VMEM((2, mom, 2 * order, order), BF16),
            pltpu.VMEM((n_src - 1, planes, order, order), BF16),
            pltpu.VMEM((n_src - 1, planes, order, order), BF16),
            pltpu.VMEM((n_snk, planes, rows, order), BF16),
            pltpu.VMEM((n_snk - 1, planes, rows, order), BF16),
            pltpu.VMEM((n_src, planes, rows, order), BF16),
            dma((n_snk - 1,)), dma((n_snk - 1,)),
            dma((5, mom)), dma((2 * mom,)),
            dma((n_src - 1,)), dma((n_src - 1,)),
            dma((n_snk - 1,)), dma((n_snk - 1,)),
            dma((n_src - 1,)), dma((n_src - 1,)),
        ],
        compiler_params=pltpu.CompilerParams(
            collective_id=0, has_side_effects=True, vmem_limit_bytes=40 * 2**20
        ),
    )(tau, blocks, *edges, weight_table)
    out = out.reshape(NODES, 2, rows, order)
    return jnp.transpose(out, (2, 0, 1, 3))


def solution(mesh):
    return jax.shard_map(
        shards,
        mesh=mesh,
        in_specs=(
            P("src", None, None, None, "snk"),
            P("snk", None, None, None, None),
            P("src", "snk", None),
            P("src", "snk", None),
            P("src", "snk", None),
            P("src", "snk", None),
            P(),
        ),
        out_specs=P("snk", None, None, None),
        check_vma=False,
    )
```
